32 devices in a mesh: dp: 4 (over y, x), seq: 8 (over z, core).
Axes of the slice: x: 2, y: 2, z: 4, core: 2. Of those that a mesh axis runs over, the one named last changes fastest.
Arguments:
- tokens_in: bfloat16 [4, 1024, 12288], P('dp', 'seq'), may hold values from -6 to 6
- short_filter: float32 [7, 12288], replicated, may hold values from -2 to 2
- long_filter: bfloat16 [256, 128], replicated, may hold values from -0.5 to 0.5
- out_weight: bfloat16 [4096, 4096], P('dp', 'seq'), may hold values from -0.09375 to 0.09375
- cotangent: bfloat16 [4, 1024, 4096], P('dp', None, 'seq'), may hold values from -6 to 6
Outputs:
- block_out: bfloat16 [4, 1024, 4096], P('dp', None, 'seq')
- grad_tokens: bfloat16 [4, 1024, 12288], P('dp', 'seq')
- grad_short: float32 [7, 12288], replicated
- grad_long: float32 [256, 128], replicated
- grad_weight: float32 [4096, 4096], P('dp', 'seq')
The draws below stay inside these ranges and needn't reach their ends.
All inputs are finite; a program needn't handle non-finite values.
Results may differ from the reference program's by a relative error of at most 0.023.
Values may be sent and summed in bfloat16 or wider, within the bound.
A program may use at most 192 MiB of HBM per device.

```python
import jax
import jax.numpy as jnp
from jax import lax

D = 4096
TAPS = 128
SHORT = 7
GROUPS = 256
SEQS = 4
LEN = 1024
N_SEQ = 8


def raised(result, stream_key, source, target, parts, factor):
    def block_of(axis_at):
        return (jnp.arange(result.shape[axis_at]) // (result.shape[axis_at] // parts)).reshape((-1,) + (1,) * (result.ndim - 1 - axis_at))

    first = jax.random.permutation(stream_key, parts)[block_of(target)]
    far = (block_of(target) + parts // 2) % parts
    return jnp.where((block_of(source) == first) | (block_of(source) == far), factor * result, result)


def shard_levels(stream_key, dims, cuts, least, largest):
    gain, own = 1.0, jax.random.fold_in(stream_key, 6)
    for axis_at, blocks in cuts:
        steps = jnp.exp(jax.random.uniform(jax.random.fold_in(own, axis_at), (blocks,), jnp.float32, least / len(cuts), largest / len(cuts)))
        gain = gain * jnp.repeat(steps, dims[axis_at] // blocks).reshape([-1 if axis == axis_at else 1 for axis in range(len(dims))])
    return gain


def centred(stream_key, dims, width, limit, pieces=(), kind=jnp.bfloat16):
    loudness = shard_levels(stream_key, dims, pieces, -0.22, 0.18) if pieces else 1.0
    drawn = jax.random.normal(stream_key, dims, jnp.float32) * width * loudness
    return jnp.minimum(jnp.maximum(drawn, -limit), limit).astype(kind)


def heavy_noise(key, shape, deviation, reach, shards, heavy, held_as=jnp.bfloat16):
    result = deviation * jax.random.normal(key, shape, jnp.float32)
    if shards:
        result = result * shard_levels(key, shape, shards, -0.22, 0.18)
    return jnp.clip(raised(result, jax.random.fold_in(key, 3), *heavy), -reach, reach).astype(held_as)


def setup_inputs(seed: int = 0) -> dict:
    seeds = jax.random.split(jax.random.key(seed), 6)
    tokens_in = centred(seeds[0], (SEQS, LEN, 3 * D), 1.0, 6.0, ((0, 4), (1, 8)))
    short_filter = centred(seeds[1], (SHORT, 3 * D), SHORT ** -0.5, 2.0, (), jnp.float32)
    long_filter = centred(seeds[2], (GROUPS, TAPS), TAPS ** -0.5, 0.5)
    out_weight = centred(seeds[3], (D, D), D ** -0.5, 0.09375, ((0, 4), (1, 8)))
    cotangent = heavy_noise(seeds[4], (SEQS, LEN, D), 1.0, 6.0, ((0, 4), (2, 8)), (2, 1, 8, 2.0))
    return dict(tokens_in=tokens_in, short_filter=short_filter, long_filter=long_filter, out_weight=out_weight, cotangent=cotangent)


def tap_table(filters, tap_index):
    tap_count = filters.shape[1]
    valid = (tap_index >= 0) & (tap_index < tap_count)
    clipped = jnp.clip(tap_index, 0, tap_count - 1).astype(jnp.int32)
    taken = jnp.take(filters, clipped, axis=1)
    return jnp.where(valid[None], taken, jnp.zeros((), filters.dtype))

def forward_table(filters):
    tap_count = filters.shape[1]
    row_pos = jnp.arange(tap_count, dtype=jnp.int32)[:, None]
    col_pos = jnp.arange(2 * tap_count, dtype=jnp.int32)[None, :]
    return tap_table(filters, row_pos + tap_count - col_pos)

def adjoint_table(filters):
    tap_count = filters.shape[1]
    row_pos = jnp.arange(tap_count, dtype=jnp.int32)[:, None]
    col_pos = jnp.arange(2 * tap_count, dtype=jnp.int32)[None, :]
    return tap_table(filters, col_pos - row_pos)

def windows(padded, row_count, tap_count, group_count):
    channels = padded.shape[1]
    blocks = row_count // tap_count
    leading = padded[:row_count].reshape(blocks, tap_count, group_count, channels // group_count)
    trailing = padded[tap_count:tap_count + row_count].reshape(blocks, tap_count, group_count, channels // group_count)
    return jnp.concatenate([leading, trailing], axis=1)

def einsum_exact(form, left, right):
    return jnp.einsum(form, left.astype(jnp.float32), right.astype(jnp.float32), precision=lax.Precision.HIGHEST)

def medium_grad(grad_in, window, tap_count, group_count):
    blocks = grad_in.shape[0] // tap_count
    grad_blocks = grad_in.reshape(blocks, tap_count, group_count, -1)
    products = einsum_exact('bigk,brgk->gir', grad_blocks, window)
    flattened = products.reshape(group_count, tap_count * 2 * tap_count)
    flattened = jnp.concatenate([flattened, jnp.zeros((group_count, tap_count), jnp.float32)], axis=1)
    skewed = flattened.reshape(group_count, tap_count, 2 * tap_count + 1)
    summed = lax.optimization_barrier(jnp.sum(skewed[:, :, 1:tap_count + 1], axis=1))
    return summed[:, ::-1]

def short_forward(extended, weights, row_count):
    short_taps = weights.shape[0]
    accumulated = jnp.zeros((row_count, extended.shape[1]), jnp.float32)
    for tap_index in range(short_taps):
        start_row = short_taps - 1 - tap_index
        accumulated = accumulated + weights[tap_index] * extended[start_row:start_row + row_count].astype(jnp.float32)
    return accumulated

def short_adjoint(extended, weights, row_count):
    short_taps = weights.shape[0]
    accumulated = jnp.zeros((row_count, extended.shape[1]), jnp.float32)
    for tap_index in range(short_taps):
        accumulated = accumulated + weights[tap_index] * extended[tap_index:tap_index + row_count].astype(jnp.float32)
    return accumulated

def short_grad(grads, extended, row_count):
    short_taps = extended.shape[0] - row_count + 1
    grads_wide = grads.astype(jnp.float32)
    pieces_list = []
    for tap_index in range(short_taps):
        start_row = short_taps - 1 - tap_index
        pieces_list.append(lax.optimization_barrier(jnp.sum(grads_wide * extended[start_row:start_row + row_count].astype(jnp.float32), axis=0)))
    return jnp.stack(pieces_list, axis=0)

def one_sequence(tokens, upstream, short_filter, long_filter, out_weight):
    seq_length = tokens.shape[0]
    channels = out_weight.shape[0]
    short_taps = short_filter.shape[0]
    tap_count = long_filter.shape[1]
    group_count = long_filter.shape[0]
    u_ext = jnp.concatenate([jnp.zeros((short_taps - 1, 3 * channels), jnp.bfloat16), tokens], axis=0)
    features = short_forward(u_ext, short_filter, seq_length)
    query_part = features[:, :channels]
    key_part = features[:, channels:2 * channels]
    value_part = features[:, 2 * channels:]
    mixer_in = (key_part * value_part).astype(jnp.bfloat16)
    padded = jnp.concatenate([jnp.zeros((tap_count, channels), jnp.bfloat16), mixer_in], axis=0)
    window = windows(padded, seq_length, tap_count, group_count)
    mixed = einsum_exact('gir,brgk->bigk', forward_table(long_filter), window).reshape(seq_length, channels)
    gated = (query_part * mixed).astype(jnp.bfloat16)
    block_out = jnp.dot(gated, out_weight, preferred_element_type=jnp.float32).astype(jnp.bfloat16)
    weight_part = lax.dot_general(gated, upstream, (((0,), (0,)), ((), ())), preferred_element_type=jnp.float32).astype(jnp.bfloat16)
    col_width = channels // N_SEQ

    def add_block(block_index, total):
        start_col = (block_index * col_width).astype(jnp.int32)
        grad_cols = lax.dynamic_slice_in_dim(upstream, start_col, col_width, 1)
        weight_cols = lax.dynamic_slice_in_dim(out_weight, start_col, col_width, 1)
        term = lax.dot_general(grad_cols, weight_cols, (((1,), (1,)), ((), ())), preferred_element_type=jnp.float32)
        term = lax.optimization_barrier(term.astype(jnp.bfloat16))
        return total + term.astype(jnp.float32)
    grad_gated = lax.fori_loop(0, N_SEQ, add_block, jnp.zeros((seq_length, channels), jnp.float32))
    grad_mixed_in = (grad_gated * query_part).astype(jnp.bfloat16)
    grad_pad = jnp.concatenate([grad_mixed_in, jnp.zeros((tap_count, channels), jnp.bfloat16)], axis=0)
    grad_window = windows(grad_pad, seq_length, tap_count, group_count)
    grad_mixer = einsum_exact('gpq,bqgk->bpgk', adjoint_table(long_filter), grad_window).reshape(seq_length, channels)
    grad_long = medium_grad(grad_mixed_in, window, tap_count, group_count)
    grad_features = jnp.concatenate([grad_gated * mixed, grad_mixer * value_part, grad_mixer * key_part], axis=1).astype(jnp.bfloat16)
    grad_ext = jnp.concatenate([grad_features, jnp.zeros((short_taps - 1, 3 * channels), jnp.bfloat16)], axis=0)
    grad_tokens = short_adjoint(grad_ext, short_filter, seq_length).astype(jnp.bfloat16)
    grad_short = short_grad(grad_features, u_ext, seq_length)
    return (block_out, grad_tokens, grad_short, grad_long, weight_part)

def reference(tokens_in, short_filter, long_filter, out_weight, cotangent):

    def per_sequence(pair):
        return one_sequence(pair[0], pair[1], short_filter, long_filter, out_weight)
    block_out, grad_tokens, short_parts, long_parts, weight_parts = lax.map(per_sequence, (tokens_in, cotangent))
    weight_parts = lax.optimization_barrier(weight_parts)
    grad_weight = lax.optimization_barrier(jnp.sum(weight_parts.astype(jnp.float32), axis=0))
    return (block_out, grad_tokens, lax.optimization_barrier(jnp.sum(short_parts, axis=0)), lax.optimization_barrier(jnp.sum(long_parts, axis=0)), grad_weight)
```

```python
import functools

import jax
import jax.numpy as jnp
from jax import lax
from jax.experimental import pallas as pl
from jax.experimental.pallas import tpu as pltpu
from jax.sharding import PartitionSpec as P

LANES = 128
HALO = 8
BF = jnp.bfloat16
F32 = jnp.float32


def shifted(x, axis, by):
    size = lax.axis_size(axis)
    pairs = [(i, i + by) for i in range(size) if 0 <= i + by < size]
    return lax.ppermute(x, axis, pairs)


def features_kernel(tok_ref, rim_ref, w_ref, feat_ref, mix_ref, ext, key):
    part = pl.program_id(1)
    rows, width = tok_ref.shape
    taps = w_ref.shape[0]

    def lane_block(b, carry):
        sl = pl.ds(pl.multiple_of(b * LANES, LANES), LANES)
        ext[0:HALO, :] = rim_ref[:, sl]
        ext[HALO : HALO + rows, :] = tok_ref[:, sl].astype(F32)
        w = w_ref[:, sl]
        acc = jnp.zeros((rows, LANES), F32)
        for j in range(taps):
            acc = acc + w[j : j + 1] * ext[HALO - j : HALO - j + rows, :]
        feat_ref[:, sl] = acc

        @pl.when(part == 1)
        def _():
            key[:, sl] = acc

        @pl.when(part == 2)
        def _():
            mix_ref[:, sl] = (acc * key[:, sl]).astype(BF)

        return carry

    lax.fori_loop(0, width // LANES, lane_block, 0)


def group_tables(filt_ref, b, per, table, lower_first):
    taps = filt_ref.shape[1]
    row = lax.broadcasted_iota(jnp.int32, (taps, taps), 0)
    col = lax.broadcasted_iota(jnp.int32, (taps, taps), 1)
    first = (col >= row) if lower_first else (col > row)
    filt = filt_ref[pl.ds(pl.multiple_of(b * per, per), per), :]
    for g in range(per):
        base = jnp.broadcast_to(filt[g : g + 1, :], (taps, taps))
        circ = pltpu.roll(base, 0, 1, stride=1, stride_axis=0)
        table[g * taps : (g + 1) * taps, 0:taps] = jnp.where(first, circ, 0.0).astype(BF)
        table[g * taps : (g + 1) * taps, taps : 2 * taps] = jnp.where(first, 0.0, circ).astype(BF)


def pick_groups(stacked, per, rows):
    size = LANES // per
    lane = lax.broadcasted_iota(jnp.int32, (rows, LANES), 1)
    out = stacked[0:rows]
    for g in range(1, per):
        out = jnp.where(lane >= g * size, stacked[g * rows : (g + 1) * rows], out)
    return out


def mixed_kernel(per, mix_ref, lead_ref, query_ref, filt_ref, mixed_ref, gated_ref, table, win):
    rows, width = mix_ref.shape

    def lane_block(b, carry):
        sl = pl.ds(pl.multiple_of(b * LANES, LANES), LANES)
        group_tables(filt_ref, b, per, table, False)
        win[0:rows, :] = lead_ref[:, sl]
        win[rows : 2 * rows, :] = mix_ref[:, sl]
        stacked = jnp.dot(table[...], win[...], preferred_element_type=F32)
        mixed = pick_groups(stacked, per, rows)
        mixed_ref[:, sl] = mixed
        gated_ref[:, sl] = (query_ref[:, sl] * mixed).astype(BF)
        return carry

    lax.fori_loop(0, width // LANES, lane_block, 0)


def backward_kernel(
    per, gg_ref, next_ref, query_ref, key_ref, value_ref, mixed_ref, mix_ref, lead_ref,
    filt_ref, tok_ref, rim_ref, w_ref,
    gtok_ref, tail_ref, head_ref, gshort_ref, glong_ref,
    table, win, masked, gf, ext,
):
    part = pl.program_id(1)
    rows, width = gg_ref.shape
    taps = w_ref.shape[0]
    size = LANES // per
    blocks = width // LANES

    @pl.when(part == 0)
    def _():
        row = lax.broadcasted_iota(jnp.int32, (rows, rows), 0)
        col = lax.broadcasted_iota(jnp.int32, (rows, rows), 1)
        flip = jnp.where(row + col == rows - 1, 1.0, 0.0).astype(BF)
        lead_side = col + row > rows - 1
        lane = lax.broadcasted_iota(jnp.int32, (rows, LANES), 1)

        def lane_block(b, carry):
            sl = pl.ds(pl.multiple_of(b * LANES, LANES), LANES)
            gg = gg_ref[:, sl].astype(F32)
            gm = (gg * query_ref[:, sl]).astype(BF)
            group_tables(filt_ref, b, per, table, True)
            win[0:rows, :] = gm
            win[rows : 2 * rows, :] = next_ref[:, sl]
            stacked = jnp.dot(table[...], win[...], preferred_element_type=F32)
            gmix = pick_groups(stacked, per, rows)
            parts = (gg * mixed_ref[:, sl], gmix * value_ref[:, sl], gmix * key_ref[:, sl])
            for p in range(3):
                gf[p, 0:rows, sl] = parts[p].astype(BF).astype(F32)
                gf[p, rows : rows + HALO, sl] = jnp.zeros((HALO, LANES), F32)
            rev = jnp.dot(flip, gm, preferred_element_type=F32)
            for g in range(per):
                mine = (lane >= g * size) & (lane < (g + 1) * size)
                masked[g * rows : (g + 1) * rows, :] = jnp.where(mine, rev, 0.0).astype(BF)
            win[0:rows, :] = lead_ref[:, sl]
            win[rows : 2 * rows, :] = mix_ref[:, sl]
            prods = lax.dot_general(
                masked[...], win[...], (((1,), (1,)), ((), ())), preferred_element_type=F32
            )
            sums = []
            for g in range(per):
                one = prods[g * rows : (g + 1) * rows]
                fold = jnp.where(lead_side, one[:, 0:rows], one[:, rows : 2 * rows])
                turned = pltpu.roll(fold, 0, 1, stride=1, stride_axis=0)
                sums.append(jnp.sum(turned, axis=0, keepdims=True))
            glong_ref[pl.ds(pl.multiple_of(b * per, per), per), :] = jnp.concatenate(sums, axis=0)
            return carry

        lax.fori_loop(0, blocks, lane_block, 0)

    def short_block(b, carry):
        sl = pl.ds(pl.multiple_of(b * LANES, LANES), LANES)
        ext[0:HALO, :] = rim_ref[:, sl]
        ext[HALO : HALO + rows, :] = tok_ref[:, sl].astype(F32)
        w = w_ref[:, sl]
        own = gf[part, 0:rows, sl]
        head_ref[:, sl] = own[0:HALO]
        acc = w[0:1] * own
        sums = [jnp.sum(own * ext[HALO : HALO + rows, :], axis=0, keepdims=True)]
        for j in range(1, taps):
            acc = acc + w[j : j + 1] * gf[part, j : j + rows, sl]
            sums.append(
                jnp.sum(own * ext[HALO - j : HALO - j + rows, :], axis=0, keepdims=True)
            )
        for _ in range(HALO - taps):
            sums.append(jnp.zeros((1, LANES), F32))
        gtok_ref[:, sl] = acc.astype(BF)
        tail_ref[:, sl] = acc[rows - HALO : rows]
        gshort_ref[:, sl] = jnp.concatenate(sums, axis=0)
        return carry

    lax.fori_loop(0, blocks, short_block, 0)


def reduce_kernel(n_dp, n_seq, x_ref, y_ref, got_dp, half, got_seq, full, s1, r1, s2, r2, s3, r3, s4, r4):
    dp = lax.axis_index("dp")
    seq = lax.axis_index("seq")
    mesh_id = pl.DeviceIdType.MESH

    def dp_peer(k):
        return (lax.rem(dp + k, n_dp), seq)

    def seq_peer(k):
        return (dp, lax.rem(seq + k, n_seq))

    barrier = pltpu.get_barrier_semaphore()
    for k in range(1, n_dp):
        pl.semaphore_signal(barrier, inc=1, device_id=dp_peer(k), device_id_type=mesh_id)
    for k in range(1, n_seq):
        pl.semaphore_signal(barrier, inc=1, device_id=seq_peer(k), device_id_type=mesh_id)
    pl.semaphore_wait(barrier, n_dp + n_seq - 2)

    def exchange(count, peer, source, target, send, recv):
        copies = []
        for k in range(1, count):
            copy = pltpu.make_async_remote_copy(
                src_ref=source(k), dst_ref=target(k), send_sem=send.at[k - 1],
                recv_sem=recv.at[k - 1], device_id=peer(k), device_id_type=mesh_id,
            )
            copy.start()
            copies.append(copy)
        for copy in copies:
            copy.wait()

    exchange(n_dp, dp_peer, lambda k: x_ref.at[lax.rem(dp + k, n_dp)],
             lambda k: got_dp.at[k - 1], s1, r1)
    total = x_ref[dp]
    for k in range(1, n_dp):
        total = total + got_dp[k - 1]
    half[...] = total
    exchange(n_seq, seq_peer, lambda k: half.at[lax.rem(seq + k, n_seq)],
             lambda k: got_seq.at[k - 1], s2, r2)
    total = half[seq]
    for k in range(1, n_seq):
        total = total + got_seq[k - 1]
    full[dp, seq] = total
    exchange(n_seq, seq_peer, lambda k: full.at[dp, seq], lambda k: full.at[dp, seq], s3, r3)
    exchange(n_dp, dp_peer, lambda k: full.at[dp], lambda k: full.at[dp], s4, r4)
    y_ref[...] = full[...]


def all_reduce_small(flat):
    n_dp, n_seq = lax.axis_size("dp"), lax.axis_size("seq")
    devices = n_dp * n_seq
    size = flat.shape[0]
    per = -(-size // (devices * 8 * LANES)) * 8
    padded = jnp.pad(flat, (0, devices * per * LANES - size))
    x = padded.reshape(n_dp, n_seq, per, LANES)
    dma = pltpu.SemaphoreType.DMA
    out = pl.pallas_call(
        functools.partial(reduce_kernel, n_dp, n_seq),
        out_shape=jax.ShapeDtypeStruct(x.shape, F32),
        in_specs=[pl.BlockSpec(memory_space=pltpu.VMEM)],
        out_specs=pl.BlockSpec(memory_space=pltpu.VMEM),
        scratch_shapes=[
            pltpu.VMEM((n_dp - 1, n_seq, per, LANES), F32),
            pltpu.VMEM((n_seq, per, LANES), F32),
            pltpu.VMEM((n_seq - 1, per, LANES), F32),
            pltpu.VMEM(x.shape, F32),
            dma((n_dp - 1,)), dma((n_dp - 1,)),
            dma((n_seq - 1,)), dma((n_seq - 1,)),
            dma((n_seq - 1,)), dma((n_seq - 1,)),
            dma((n_dp - 1,)), dma((n_dp - 1,)),
        ],
        compiler_params=pltpu.CompilerParams(
            collective_id=0, has_side_effects=True, vmem_limit_bytes=16 << 20
        ),
        cost_estimate=pl.CostEstimate(flops=size, bytes_accessed=8 * size, transcendentals=0),
    )(x)
    return out.reshape(-1)[:size]


def shards(tokens_in, short_filter, long_filter, out_weight, cotangent):
    tokens = tokens_in[0]
    row_count = tokens.shape[0]
    channels = tokens.shape[1] // 3
    short_taps = short_filter.shape[0]
    group_count, tap_count = long_filter.shape
    per = LANES * group_count // channels
    width = min(1024, channels)
    nb = channels // width
    groups = group_count // nb
    limit = 40 << 20

    weights = lax.all_gather(out_weight, "dp", axis=0, tiled=True)
    upstream = cotangent[0]
    rim = shifted(tokens[row_count - HALO :], "seq", 1).astype(F32)
    filt = long_filter.astype(F32)
    turned = jnp.roll(filt[:, ::-1], 1, axis=1)

    by_part = lambda rows: pl.BlockSpec((rows, width), lambda j, p: (0, p * nb + j))
    features, mixer_in = pl.pallas_call(
        features_kernel,
        grid=(nb, 3),
        in_specs=[by_part(row_count), by_part(HALO), by_part(short_taps)],
        out_specs=[by_part(row_count), pl.BlockSpec((row_count, width), lambda j, p: (0, j))],
        out_shape=[
            jax.ShapeDtypeStruct((row_count, 3 * channels), F32),
            jax.ShapeDtypeStruct((row_count, channels), BF),
        ],
        scratch_shapes=[
            pltpu.VMEM((row_count + HALO, LANES), F32),
            pltpu.VMEM((row_count, width), F32),
        ],
        compiler_params=pltpu.CompilerParams(vmem_limit_bytes=limit),
        cost_estimate=pl.CostEstimate(
            flops=42 * row_count * channels, bytes_accessed=20 * row_count * channels, transcendentals=0
        ),
    )(tokens, rim, short_filter)
    lead = shifted(mixer_in, "seq", 1)

    col = lambda off: pl.BlockSpec((row_count, width), lambda j: (0, off * nb + j))
    mixed, gated = pl.pallas_call(
        functools.partial(mixed_kernel, per),
        grid=(nb,),
        in_specs=[col(0), col(0), col(0), pl.BlockSpec((groups, tap_count), lambda j: (j, 0))],
        out_specs=[col(0), col(0)],
        out_shape=[
            jax.ShapeDtypeStruct((row_count, channels), F32),
            jax.ShapeDtypeStruct((row_count, channels), BF),
        ],
        scratch_shapes=[
            pltpu.VMEM((per * tap_count, 2 * tap_count), BF),
            pltpu.VMEM((2 * tap_count, LANES), BF),
        ],
        compiler_params=pltpu.CompilerParams(vmem_limit_bytes=limit),
        cost_estimate=pl.CostEstimate(
            flops=4 * per * tap_count * row_count * channels,
            bytes_accessed=14 * row_count * channels, transcendentals=0,
        ),
    )(mixer_in, lead, features, turned)

    all_rows = lax.all_gather(gated, "seq", axis=0, tiled=True)
    grad_gated = lax.psum_scatter(
        lax.dot_general(
            upstream, weights, (((1,), (1,)), ((), ())), preferred_element_type=F32
        ).astype(BF),
        "seq",
        scatter_dimension=0,
        tiled=True,
    )
    weight_grad = lax.dot_general(
        all_rows, upstream, (((0,), (0,)), ((), ())), preferred_element_type=F32
    )
    grad_weight = lax.psum_scatter(
        weight_grad.astype(BF), "dp", scatter_dimension=0, tiled=True
    ).astype(F32)
    output = jnp.dot(all_rows, weights, preferred_element_type=F32).astype(BF)

    grad_mixed_in = (grad_gated.astype(F32) * features[:, :channels]).astype(BF)
    grad_next = shifted(grad_mixed_in, "seq", -1)
    at = lambda off: pl.BlockSpec((row_count, width), lambda j, p: (0, off * nb + j))
    group_spec = pl.BlockSpec((groups, tap_count), lambda j, p: (j, 0))
    grad_tokens, tail, head, short_local, long_local = pl.pallas_call(
        functools.partial(backward_kernel, per),
        grid=(nb, 3),
        in_specs=[
            at(0), at(0), at(0), at(1), at(2), at(0), at(0), at(0), group_spec,
            by_part(row_count), by_part(HALO), by_part(short_taps),
        ],
        out_specs=[by_part(row_count), by_part(HALO), by_part(HALO), by_part(HALO), group_spec],
        out_shape=[
            jax.ShapeDtypeStruct((row_count, 3 * channels), BF),
            jax.ShapeDtypeStruct((HALO, 3 * channels), F32),
            jax.ShapeDtypeStruct((HALO, 3 * channels), F32),
            jax.ShapeDtypeStruct((HALO, 3 * channels), F32),
            jax.ShapeDtypeStruct((group_count, tap_count), F32),
        ],
        scratch_shapes=[
            pltpu.VMEM((per * tap_count, 2 * tap_count), BF),
            pltpu.VMEM((2 * tap_count, LANES), BF),
            pltpu.VMEM((per * row_count, LANES), BF),
            pltpu.VMEM((3, row_count + HALO, width), F32),
            pltpu.VMEM((row_count + HALO, LANES), F32),
        ],
        compiler_params=pltpu.CompilerParams(vmem_limit_bytes=limit),
        cost_estimate=pl.CostEstimate(
            flops=8 * per * tap_count * row_count * channels,
            bytes_accessed=40 * row_count * channels, transcendentals=0,
        ),
    )(
        grad_gated, grad_next, features, features, features, mixed, mixer_in, lead, filt,
        tokens, rim, short_filter,
    )

    follow = shifted(head.astype(BF), "seq", -1).astype(F32)
    beyond = jnp.concatenate([jnp.zeros_like(follow), follow], axis=0)
    for j in range(short_taps):
        tail = tail + short_filter[j] * beyond[j : j + HALO]
    grad_tokens = lax.dynamic_update_slice(grad_tokens, tail.astype(BF), (row_count - HALO, 0))

    summed = all_reduce_small(
        jnp.concatenate([short_local.reshape(-1), long_local.reshape(-1)])
    )
    cut = HALO * 3 * channels
    grad_short = summed[:cut].reshape(HALO, 3 * channels)[:short_taps]
    grad_long = summed[cut:].reshape(group_count, tap_count)[:, ::-1]
    return (output[None], grad_tokens[None], grad_short, grad_long, grad_weight)


def solution(mesh):
    return jax.shard_map(
        shards,
        mesh=mesh,
        in_specs=(P("dp", "seq", None), P(), P(), P("dp", "seq"), P("dp", None, "seq")),
        out_specs=(P("dp", None, "seq"), P("dp", "seq", None), P(), P(), P("dp", "seq")),
        check_vma=False,
    )
```

```python
import functools

import jax
import jax.numpy as jnp
from jax import lax
from jax.experimental import pallas as pl
from jax.experimental.pallas import tpu as pltpu
from jax.sharding import PartitionSpec as P

LANES = 128
HALO = 8
BF = jnp.bfloat16
F32 = jnp.float32


def shifted(x, axis, by):
    size = lax.axis_size(axis)
    pairs = [(i, i + by) for i in range(size) if 0 <= i + by < size]
    return lax.ppermute(x, axis, pairs)


def features_kernel(tok_ref, rim_ref, w_ref, feat_ref, mix_ref, ext, key):
    part = pl.program_id(1)
    rows, width = tok_ref.shape
    taps = w_ref.shape[0]

    def lane_block(b, carry):
        sl = pl.ds(pl.multiple_of(b * LANES, LANES), LANES)
        ext[0:HALO, :] = rim_ref[:, sl]
        ext[HALO : HALO + rows, :] = tok_ref[:, sl].astype(F32)
        w = w_ref[:, sl]
        acc = jnp.zeros((rows, LANES), F32)
        for j in range(taps):
            acc = acc + w[j : j + 1] * ext[HALO - j : HALO - j + rows, :]
        feat_ref[:, sl] = acc

        @pl.when(part == 1)
        def _():
            key[:, sl] = acc

        @pl.when(part == 2)
        def _():
            mix_ref[:, sl] = (acc * key[:, sl]).astype(BF)

        return carry

    lax.fori_loop(0, width // LANES, lane_block, 0)


def group_tables(filt_ref, b, per, table, lower_first):
    taps = filt_ref.shape[1]
    row = lax.broadcasted_iota(jnp.int32, (taps, taps), 0)
    col = lax.broadcasted_iota(jnp.int32, (taps, taps), 1)
    first = (col >= row) if lower_first else (col > row)
    filt = filt_ref[pl.ds(pl.multiple_of(b * per, per), per), :]
    for g in range(per):
        base = jnp.broadcast_to(filt[g : g + 1, :], (taps, taps))
        circ = pltpu.roll(base, 0, 1, stride=1, stride_axis=0)
        table[g * taps : (g + 1) * taps, 0:taps] = jnp.where(first, circ, 0.0).astype(BF)
        table[g * taps : (g + 1) * taps, taps : 2 * taps] = jnp.where(first, 0.0, circ).astype(BF)


def pick_groups(stacked, per, rows):
    size = LANES // per
    lane = lax.broadcasted_iota(jnp.int32, (rows, LANES), 1)
    out = stacked[0:rows]
    for g in range(1, per):
        out = jnp.where(lane >= g * size, stacked[g * rows : (g + 1) * rows], out)
    return out


def mixed_kernel(per, mix_ref, lead_ref, query_ref, filt_ref, mixed_ref, gated_ref, table, win):
    rows, width = mix_ref.shape

    def lane_block(b, carry):
        sl = pl.ds(pl.multiple_of(b * LANES, LANES), LANES)
        group_tables(filt_ref, b, per, table, False)
        win[0:rows, :] = lead_ref[:, sl]
        win[rows : 2 * rows, :] = mix_ref[:, sl]
        stacked = jnp.dot(table[...], win[...], preferred_element_type=F32)
        mixed = pick_groups(stacked, per, rows)
        mixed_ref[:, sl] = mixed
        gated_ref[:, sl] = (query_ref[:, sl] * mixed).astype(BF)
        return carry

    lax.fori_loop(0, width // LANES, lane_block, 0)


def backward_kernel(
    per, gg_ref, next_ref, query_ref, key_ref, value_ref, mixed_ref, mix_ref, lead_ref,
    filt_ref, tok_ref, rim_ref, w_ref,
    gtok_ref, tail_ref, head_ref, gshort_ref, glong_ref,
    table, win, masked, gf, ext,
):
    part = pl.program_id(1)
    rows, width = gg_ref.shape
    taps = w_ref.shape[0]
    size = LANES // per
    blocks = width // LANES

    @pl.when(part == 0)
    def _():
        row = lax.broadcasted_iota(jnp.int32, (rows, rows), 0)
        col = lax.broadcasted_iota(jnp.int32, (rows, rows), 1)
        flip = jnp.where(row + col == rows - 1, 1.0, 0.0).astype(BF)
        lead_side = col + row > rows - 1
        lane = lax.broadcasted_iota(jnp.int32, (rows, LANES), 1)

        def lane_block(b, carry):
            sl = pl.ds(pl.multiple_of(b * LANES, LANES), LANES)
            gg = gg_ref[:, sl]
            gm = (gg * query_ref[:, sl]).astype(BF)
            group_tables(filt_ref, b, per, table, True)
            win[0:rows, :] = gm
            win[rows : 2 * rows, :] = next_ref[:, sl]
            stacked = jnp.dot(table[...], win[...], preferred_element_type=F32)
            gmix = pick_groups(stacked, per, rows)
            parts = (gg * mixed_ref[:, sl], gmix * value_ref[:, sl], gmix * key_ref[:, sl])
            for p in range(3):
                gf[p, 0:rows, sl] = parts[p].astype(BF).astype(F32)
                gf[p, rows : rows + HALO, sl] = jnp.zeros((HALO, LANES), F32)
            rev = jnp.dot(flip, gm, preferred_element_type=F32)
            for g in range(per):
                mine = (lane >= g * size) & (lane < (g + 1) * size)
                masked[g * rows : (g + 1) * rows, :] = jnp.where(mine, rev, 0.0).astype(BF)
            win[0:rows, :] = lead_ref[:, sl]
            win[rows : 2 * rows, :] = mix_ref[:, sl]
            prods = lax.dot_general(
                masked[...], win[...], (((1,), (1,)), ((), ())), preferred_element_type=F32
            )
            sums = []
            for g in range(per):
                one = prods[g * rows : (g + 1) * rows]
                fold = jnp.where(lead_side, one[:, 0:rows], one[:, rows : 2 * rows])
                turned = pltpu.roll(fold, 0, 1, stride=1, stride_axis=0)
                sums.append(jnp.sum(turned, axis=0, keepdims=True))
            glong_ref[pl.ds(pl.multiple_of(b * per, per), per), :] = jnp.concatenate(sums, axis=0)
            return carry

        lax.fori_loop(0, blocks, lane_block, 0)

    def short_block(b, carry):
        sl = pl.ds(pl.multiple_of(b * LANES, LANES), LANES)
        ext[0:HALO, :] = rim_ref[:, sl]
        ext[HALO : HALO + rows, :] = tok_ref[:, sl].astype(F32)
        w = w_ref[:, sl]
        own = gf[part, 0:rows, sl]
        head_ref[:, sl] = own[0:HALO]
        acc = w[0:1] * own
        sums = [jnp.sum(own * ext[HALO : HALO + rows, :], axis=0, keepdims=True)]
        for j in range(1, taps):
            acc = acc + w[j : j + 1] * gf[part, j : j + rows, sl]
            sums.append(
                jnp.sum(own * ext[HALO - j : HALO - j + rows, :], axis=0, keepdims=True)
            )
        for _ in range(HALO - taps):
            sums.append(jnp.zeros((1, LANES), F32))
        gtok_ref[:, sl] = acc.astype(BF)
        tail_ref[:, sl] = acc[rows - HALO : rows]
        gshort_ref[:, sl] = jnp.concatenate(sums, axis=0)
        return carry

    lax.fori_loop(0, blocks, short_block, 0)


def reduce_kernel(n_dp, n_seq, x_ref, y_ref, got_dp, half, got_seq, full, s1, r1, s2, r2, s3, r3, s4, r4):
    dp = lax.axis_index("dp")
    seq = lax.axis_index("seq")
    mesh_id = pl.DeviceIdType.MESH

    def dp_peer(k):
        return (lax.rem(dp + k, n_dp), seq)

    def seq_peer(k):
        return (dp, lax.rem(seq + k, n_seq))

    barrier = pltpu.get_barrier_semaphore()
    for k in range(1, n_dp):
        pl.semaphore_signal(barrier, inc=1, device_id=dp_peer(k), device_id_type=mesh_id)
    for k in range(1, n_seq):
        pl.semaphore_signal(barrier, inc=1, device_id=seq_peer(k), device_id_type=mesh_id)
    pl.semaphore_wait(barrier, n_dp + n_seq - 2)

    def exchange(count, peer, source, target, send, recv):
        copies = []
        for k in range(1, count):
            copy = pltpu.make_async_remote_copy(
                src_ref=source(k), dst_ref=target(k), send_sem=send.at[k - 1],
                recv_sem=recv.at[k - 1], device_id=peer(k), device_id_type=mesh_id,
            )
            copy.start()
            copies.append(copy)
        for copy in copies:
            copy.wait()

    exchange(n_dp, dp_peer, lambda k: x_ref.at[lax.rem(dp + k, n_dp)],
             lambda k: got_dp.at[k - 1], s1, r1)
    total = x_ref[dp]
    for k in range(1, n_dp):
        total = total + got_dp[k - 1]
    half[...] = total
    exchange(n_seq, seq_peer, lambda k: half.at[lax.rem(seq + k, n_seq)],
             lambda k: got_seq.at[k - 1], s2, r2)
    total = half[seq]
    for k in range(1, n_seq):
        total = total + got_seq[k - 1]
    full[dp, seq] = total
    exchange(n_seq, seq_peer, lambda k: full.at[dp, seq], lambda k: full.at[dp, seq], s3, r3)
    exchange(n_dp, dp_peer, lambda k: full.at[dp], lambda k: full.at[dp], s4, r4)
    y_ref[...] = full[...]


def line_kernel(n_seq, p_ref, out_ref, own, pair, from_left, from_right,
                load_sem, pair_send, pair_recv, right_send, right_recv, left_send, left_recv):
    dp = lax.axis_index("dp")
    seq = lax.axis_index("seq")
    chips = n_seq // 2
    chip, core = lax.div(seq, 2), lax.rem(seq, 2)
    pieces = right_send.shape[1]
    rows = own.shape[1] // pieces
    mesh_id = pl.DeviceIdType.MESH
    ahead = 2

    def at(other_chip, other_core):
        return (dp, other_chip * 2 + other_core)

    sibling = at(chip, 1 - core)
    right = at(lax.rem(chip + 1, chips), core)
    left = at(lax.rem(chip + chips - 1, chips), core)
    barrier = pltpu.get_barrier_semaphore()
    for peer in (sibling, right, left):
        pl.semaphore_signal(barrier, inc=1, device_id=peer, device_id_type=mesh_id)
    pl.semaphore_wait(barrier, 3)

    order = []
    for s in range(chips):
        for c in (chips - 1 - s, s):
            if c not in order:
                order.append(c)
    swaps, loads = {}, {}
    for c in order:
        swaps[c] = pltpu.make_async_remote_copy(
            src_ref=p_ref.at[c, 1 - core], dst_ref=pair.at[c], send_sem=pair_send.at[c],
            recv_sem=pair_recv.at[c], device_id=sibling, device_id_type=mesh_id,
        )
        swaps[c].start()
        loads[c] = pltpu.make_async_copy(p_ref.at[c, core], own.at[c], load_sem.at[c])
        loads[c].start()

    def piece(k):
        return pl.ds(k * rows, rows)

    def hop(rightward, c, k):
        send, recv, dst, peer = (
            (right_send, right_recv, from_left, right)
            if rightward
            else (left_send, left_recv, from_right, left)
        )
        return pltpu.make_async_remote_copy(
            src_ref=own.at[c, piece(k)], dst_ref=dst.at[c, piece(k)], send_sem=send.at[c, k],
            recv_sem=recv.at[c, k], device_id=peer, device_id_type=mesh_id,
        )

    steps = [(s, k) for s in range(chips - 1) for k in range(pieces)]
    ready = set()

    def target(rightward, s):
        return chips - 1 - s if rightward else s

    def valid(rightward, s):
        return target(rightward, s) > chip if rightward else target(rightward, s) < chip

    for n, (s, k) in enumerate(steps):
        for rightward in (True, False):
            c = target(rightward, s)
            if c not in ready:
                ready.add(c)
                loads[c].wait()
                swaps[c].wait()

            @pl.when(valid(rightward, s))
            def _():
                sl = piece(k)
                inbox = from_left if rightward else from_right
                inner = chip > 0 if rightward else chip < chips - 1
                both = own[c, sl].astype(F32) + pair[c, sl].astype(F32)

                @pl.when(inner)
                def _():
                    hop(rightward, c, k).wait_recv()
                    own[c, sl] = (both + inbox[c, sl].astype(F32)).astype(BF)

                @pl.when(jnp.logical_not(inner))
                def _():
                    own[c, sl] = both.astype(BF)

                if n >= ahead:
                    before, piece_before = steps[n - ahead]
                    hop(rightward, target(rightward, before), piece_before).wait_send()
                hop(rightward, c, k).start()

    for c in order:
        if c not in ready:
            ready.add(c)
            loads[c].wait()
            swaps[c].wait()
    for c in range(chips):

        @pl.when(chip == c)
        def _():
            for k in range(pieces):
                sl = piece(k)
                out_ref[sl, :] = own[c, sl].astype(F32) + pair[c, sl].astype(F32)
                if c > 0:
                    hop(True, c, k).wait_recv()
                    out_ref[sl, :] += from_left[c, sl].astype(F32)
                if c < chips - 1:
                    hop(False, c, k).wait_recv()
                    out_ref[sl, :] += from_right[c, sl].astype(F32)
            for rightward in (True, False):
                sent = chips - 1 - c if rightward else c
                count = sent * pieces
                for n in range(max(0, count - ahead), count):
                    s, k = steps[n]
                    hop(rightward, target(rightward, s), k).wait_send()


def sum_over_line(partial, row_count):
    n_seq = lax.axis_size("seq")
    chips = n_seq // 2
    channels = partial.shape[1]
    pieces = max(1, row_count // 32)
    dma = pltpu.SemaphoreType.DMA
    slots = pltpu.VMEM((chips, row_count, channels), BF)
    return pl.pallas_call(
        functools.partial(line_kernel, n_seq),
        out_shape=jax.ShapeDtypeStruct((row_count, channels), F32),
        in_specs=[pl.BlockSpec(memory_space=pl.ANY)],
        out_specs=pl.BlockSpec(memory_space=pltpu.VMEM),
        scratch_shapes=[
            slots, slots, slots, slots,
            dma((chips,)), dma((chips,)), dma((chips,)),
            dma((chips, pieces)), dma((chips, pieces)),
            dma((chips, pieces)), dma((chips, pieces)),
        ],
        compiler_params=pltpu.CompilerParams(
            collective_id=1, has_side_effects=True, vmem_limit_bytes=48 << 20
        ),
        cost_estimate=pl.CostEstimate(
            flops=8 * row_count * channels, bytes_accessed=300_000_000, transcendentals=0
        ),
    )(partial.reshape(chips, 2, row_count, channels))


def all_reduce_small(flat):
    n_dp, n_seq = lax.axis_size("dp"), lax.axis_size("seq")
    devices = n_dp * n_seq
    size = flat.shape[0]
    per = -(-size // (devices * 8 * LANES)) * 8
    padded = jnp.pad(flat, (0, devices * per * LANES - size))
    x = padded.reshape(n_dp, n_seq, per, LANES)
    dma = pltpu.SemaphoreType.DMA
    out = pl.pallas_call(
        functools.partial(reduce_kernel, n_dp, n_seq),
        out_shape=jax.ShapeDtypeStruct(x.shape, F32),
        in_specs=[pl.BlockSpec(memory_space=pltpu.VMEM)],
        out_specs=pl.BlockSpec(memory_space=pltpu.VMEM),
        scratch_shapes=[
            pltpu.VMEM((n_dp - 1, n_seq, per, LANES), F32),
            pltpu.VMEM((n_seq, per, LANES), F32),
            pltpu.VMEM((n_seq - 1, per, LANES), F32),
            pltpu.VMEM(x.shape, F32),
            dma((n_dp - 1,)), dma((n_dp - 1,)),
            dma((n_seq - 1,)), dma((n_seq - 1,)),
            dma((n_seq - 1,)), dma((n_seq - 1,)),
            dma((n_dp - 1,)), dma((n_dp - 1,)),
        ],
        compiler_params=pltpu.CompilerParams(
            collective_id=0, has_side_effects=True, vmem_limit_bytes=16 << 20
        ),
        cost_estimate=pl.CostEstimate(flops=size, bytes_accessed=8 * size, transcendentals=0),
    )(x)
    return out.reshape(-1)[:size]


def shards(tokens_in, short_filter, long_filter, out_weight, cotangent):
    tokens = tokens_in[0]
    row_count = tokens.shape[0]
    channels = tokens.shape[1] // 3
    short_taps = short_filter.shape[0]
    group_count, tap_count = long_filter.shape
    per = LANES * group_count // channels
    width = min(1024, channels)
    nb = channels // width
    groups = group_count // nb
    limit = 40 << 20

    weights = lax.all_gather(out_weight, "dp", axis=0, tiled=True)
    upstream = cotangent[0]
    rim = shifted(tokens[row_count - HALO :], "seq", 1).astype(F32)
    filt = long_filter.astype(F32)
    turned = jnp.roll(filt[:, ::-1], 1, axis=1)

    by_part = lambda rows: pl.BlockSpec((rows, width), lambda j, p: (0, p * nb + j))
    features, mixer_in = pl.pallas_call(
        features_kernel,
        grid=(nb, 3),
        in_specs=[by_part(row_count), by_part(HALO), by_part(short_taps)],
        out_specs=[by_part(row_count), pl.BlockSpec((row_count, width), lambda j, p: (0, j))],
        out_shape=[
            jax.ShapeDtypeStruct((row_count, 3 * channels), F32),
            jax.ShapeDtypeStruct((row_count, channels), BF),
        ],
        scratch_shapes=[
            pltpu.VMEM((row_count + HALO, LANES), F32),
            pltpu.VMEM((row_count, width), F32),
        ],
        compiler_params=pltpu.CompilerParams(vmem_limit_bytes=limit),
        cost_estimate=pl.CostEstimate(
            flops=42 * row_count * channels, bytes_accessed=20 * row_count * channels, transcendentals=0
        ),
    )(tokens, rim, short_filter)
    lead = shifted(mixer_in, "seq", 1)

    col = lambda off: pl.BlockSpec((row_count, width), lambda j: (0, off * nb + j))
    mixed, gated = pl.pallas_call(
        functools.partial(mixed_kernel, per),
        grid=(nb,),
        in_specs=[col(0), col(0), col(0), pl.BlockSpec((groups, tap_count), lambda j: (j, 0))],
        out_specs=[col(0), col(0)],
        out_shape=[
            jax.ShapeDtypeStruct((row_count, channels), F32),
            jax.ShapeDtypeStruct((row_count, channels), BF),
        ],
        scratch_shapes=[
            pltpu.VMEM((per * tap_count, 2 * tap_count), BF),
            pltpu.VMEM((2 * tap_count, LANES), BF),
        ],
        compiler_params=pltpu.CompilerParams(vmem_limit_bytes=limit),
        cost_estimate=pl.CostEstimate(
            flops=4 * per * tap_count * row_count * channels,
            bytes_accessed=14 * row_count * channels, transcendentals=0,
        ),
    )(mixer_in, lead, features, turned)

    all_rows = lax.all_gather(gated, "seq", axis=0, tiled=True)
    grad_gated = sum_over_line(
        lax.dot_general(
            upstream, weights, (((1,), (1,)), ((), ())), preferred_element_type=F32
        ).astype(BF),
        row_count,
    )
    weight_grad = lax.dot_general(
        all_rows, upstream, (((0,), (0,)), ((), ())), preferred_element_type=F32
    )
    grad_weight = lax.psum_scatter(
        weight_grad.astype(BF), "dp", scatter_dimension=0, tiled=True
    ).astype(F32)
    output = jnp.dot(all_rows, weights, preferred_element_type=F32).astype(BF)

    grad_mixed_in = (grad_gated * features[:, :channels]).astype(BF)
    grad_next = shifted(grad_mixed_in, "seq", -1)
    at = lambda off: pl.BlockSpec((row_count, width), lambda j, p: (0, off * nb + j))
    group_spec = pl.BlockSpec((groups, tap_count), lambda j, p: (j, 0))
    grad_tokens, tail, head, short_local, long_local = pl.pallas_call(
        functools.partial(backward_kernel, per),
        grid=(nb, 3),
        in_specs=[
            at(0), at(0), at(0), at(1), at(2), at(0), at(0), at(0), group_spec,
            by_part(row_count), by_part(HALO), by_part(short_taps),
        ],
        out_specs=[by_part(row_count), by_part(HALO), by_part(HALO), by_part(HALO), group_spec],
        out_shape=[
            jax.ShapeDtypeStruct((row_count, 3 * channels), BF),
            jax.ShapeDtypeStruct((HALO, 3 * channels), F32),
            jax.ShapeDtypeStruct((HALO, 3 * channels), F32),
            jax.ShapeDtypeStruct((HALO, 3 * channels), F32),
            jax.ShapeDtypeStruct((group_count, tap_count), F32),
        ],
        scratch_shapes=[
            pltpu.VMEM((per * tap_count, 2 * tap_count), BF),
            pltpu.VMEM((2 * tap_count, LANES), BF),
            pltpu.VMEM((per * row_count, LANES), BF),
            pltpu.VMEM((3, row_count + HALO, width), F32),
            pltpu.VMEM((row_count + HALO, LANES), F32),
        ],
        compiler_params=pltpu.CompilerParams(vmem_limit_bytes=limit),
        cost_estimate=pl.CostEstimate(
            flops=8 * per * tap_count * row_count * channels,
            bytes_accessed=40 * row_count * channels, transcendentals=0,
        ),
    )(
        grad_gated, grad_next, features, features, features, mixed, mixer_in, lead, filt,
        tokens, rim, short_filter,
    )

    follow = shifted(head.astype(BF), "seq", -1).astype(F32)
    beyond = jnp.concatenate([jnp.zeros_like(follow), follow], axis=0)
    for j in range(short_taps):
        tail = tail + short_filter[j] * beyond[j : j + HALO]
    grad_tokens = lax.dynamic_update_slice(grad_tokens, tail.astype(BF), (row_count - HALO, 0))

    summed = all_reduce_small(
        jnp.concatenate([short_local.reshape(-1), long_local.reshape(-1)])
    )
    cut = HALO * 3 * channels
    grad_short = summed[:cut].reshape(HALO, 3 * channels)[:short_taps]
    grad_long = summed[cut:].reshape(group_count, tap_count)[:, ::-1]
    return (output[None], grad_tokens[None], grad_short, grad_long, grad_weight)


def solution(mesh):
    return jax.shard_map(
        shards,
        mesh=mesh,
        in_specs=(P("dp", "seq", None), P(), P(), P("dp", "seq"), P("dp", None, "seq")),
        out_specs=(P("dp", None, "seq"), P("dp", "seq", None), P(), P(), P("dp", "seq")),
        check_vma=False,
    )
```

```python
import functools

import jax
import jax.numpy as jnp
from jax import lax
from jax.experimental import pallas as pl
from jax.experimental.pallas import tpu as pltpu
from jax.sharding import PartitionSpec as P

LANES = 128
HALO = 8
BF = jnp.bfloat16
F32 = jnp.float32


def shifted(x, axis, by):
    size = lax.axis_size(axis)
    pairs = [(i, i + by) for i in range(size) if 0 <= i + by < size]
    return lax.ppermute(x, axis, pairs)


def features_kernel(tok_ref, rim_ref, w_ref, feat_ref, mix_ref, ext, key):
    part = pl.program_id(1)
    rows, width = tok_ref.shape
    taps = w_ref.shape[0]

    def lane_block(b, carry):
        sl = pl.ds(pl.multiple_of(b * LANES, LANES), LANES)
        ext[0:HALO, :] = rim_ref[:, sl]
        ext[HALO : HALO + rows, :] = tok_ref[:, sl].astype(F32)
        w = w_ref[:, sl]
        acc = jnp.zeros((rows, LANES), F32)
        for j in range(taps):
            acc = acc + w[j : j + 1] * ext[HALO - j : HALO - j + rows, :]
        feat_ref[:, sl] = acc

        @pl.when(part == 1)
        def _():
            key[:, sl] = acc

        @pl.when(part == 2)
        def _():
            mix_ref[:, sl] = (acc * key[:, sl]).astype(BF)

        return carry

    lax.fori_loop(0, width // LANES, lane_block, 0)


def group_tables(filt_ref, b, per, table, lower_first):
    taps = filt_ref.shape[1]
    row = lax.broadcasted_iota(jnp.int32, (taps, taps), 0)
    col = lax.broadcasted_iota(jnp.int32, (taps, taps), 1)
    first = (col >= row) if lower_first else (col > row)
    filt = filt_ref[pl.ds(pl.multiple_of(b * per, per), per), :]
    for g in range(per):
        base = jnp.broadcast_to(filt[g : g + 1, :], (taps, taps))
        circ = pltpu.roll(base, 0, 1, stride=1, stride_axis=0)
        table[g * taps : (g + 1) * taps, 0:taps] = jnp.where(first, circ, 0.0).astype(BF)
        table[g * taps : (g + 1) * taps, taps : 2 * taps] = jnp.where(first, 0.0, circ).astype(BF)


def pick_groups(stacked, per, rows):
    size = LANES // per
    lane = lax.broadcasted_iota(jnp.int32, (rows, LANES), 1)
    out = stacked[0:rows]
    for g in range(1, per):
        out = jnp.where(lane >= g * size, stacked[g * rows : (g + 1) * rows], out)
    return out


def mixed_kernel(per, mix_ref, lead_ref, query_ref, filt_ref, mixed_ref, gated_ref, table, win):
    rows, width = mix_ref.shape

    def lane_block(b, carry):
        sl = pl.ds(pl.multiple_of(b * LANES, LANES), LANES)
        group_tables(filt_ref, b, per, table, False)
        win[0:rows, :] = lead_ref[:, sl]
        win[rows : 2 * rows, :] = mix_ref[:, sl]
        stacked = jnp.dot(table[...], win[...], preferred_element_type=F32)
        mixed = pick_groups(stacked, per, rows)
        mixed_ref[:, sl] = mixed
        gated_ref[:, sl] = (query_ref[:, sl] * mixed).astype(BF)
        return carry

    lax.fori_loop(0, width // LANES, lane_block, 0)


def backward_kernel(
    per, gg_ref, next_ref, query_ref, key_ref, value_ref, mixed_ref, mix_ref, lead_ref,
    filt_ref, tok_ref, rim_ref, w_ref,
    gtok_ref, tail_ref, head_ref, gshort_ref, glong_ref,
    table, win, masked, gf, ext,
):
    part = pl.program_id(1)
    rows, width = gg_ref.shape
    taps = w_ref.shape[0]
    size = LANES // per
    blocks = width // LANES

    @pl.when(part == 0)
    def _():
        row = lax.broadcasted_iota(jnp.int32, (rows, rows), 0)
        col = lax.broadcasted_iota(jnp.int32, (rows, rows), 1)
        flip = jnp.where(row + col == rows - 1, 1.0, 0.0).astype(BF)
        lead_side = col + row > rows - 1
        lane = lax.broadcasted_iota(jnp.int32, (rows, LANES), 1)

        def lane_block(b, carry):
            sl = pl.ds(pl.multiple_of(b * LANES, LANES), LANES)
            gg = gg_ref[:, sl]
            gm = (gg * query_ref[:, sl]).astype(BF)
            group_tables(filt_ref, b, per, table, True)
            win[0:rows, :] = gm
            win[rows : 2 * rows, :] = next_ref[:, sl]
            stacked = jnp.dot(table[...], win[...], preferred_element_type=F32)
            gmix = pick_groups(stacked, per, rows)
            parts = (gg * mixed_ref[:, sl], gmix * value_ref[:, sl], gmix * key_ref[:, sl])
            for p in range(3):
                gf[p, 0:rows, sl] = parts[p].astype(BF).astype(F32)
                gf[p, rows : rows + HALO, sl] = jnp.zeros((HALO, LANES), F32)
            rev = jnp.dot(flip, gm, preferred_element_type=F32)
            for g in range(per):
                mine = (lane >= g * size) & (lane < (g + 1) * size)
                masked[g * rows : (g + 1) * rows, :] = jnp.where(mine, rev, 0.0).astype(BF)
            win[0:rows, :] = lead_ref[:, sl]
            win[rows : 2 * rows, :] = mix_ref[:, sl]
            prods = lax.dot_general(
                masked[...], win[...], (((1,), (1,)), ((), ())), preferred_element_type=F32
            )
            sums = []
            for g in range(per):
                one = prods[g * rows : (g + 1) * rows]
                fold = jnp.where(lead_side, one[:, 0:rows], one[:, rows : 2 * rows])
                turned = pltpu.roll(fold, 0, 1, stride=1, stride_axis=0)
                sums.append(jnp.sum(turned, axis=0, keepdims=True))
            glong_ref[pl.ds(pl.multiple_of(b * per, per), per), :] = jnp.concatenate(sums, axis=0)
            return carry

        lax.fori_loop(0, blocks, lane_block, 0)

    def short_block(b, carry):
        sl = pl.ds(pl.multiple_of(b * LANES, LANES), LANES)
        ext[0:HALO, :] = rim_ref[:, sl]
        ext[HALO : HALO + rows, :] = tok_ref[:, sl].astype(F32)
        w = w_ref[:, sl]
        own = gf[part, 0:rows, sl]
        head_ref[:, sl] = own[0:HALO]
        acc = w[0:1] * own
        sums = [jnp.sum(own * ext[HALO : HALO + rows, :], axis=0, keepdims=True)]
        for j in range(1, taps):
            acc = acc + w[j : j + 1] * gf[part, j : j + rows, sl]
            sums.append(
                jnp.sum(own * ext[HALO - j : HALO - j + rows, :], axis=0, keepdims=True)
            )
        for _ in range(HALO - taps):
            sums.append(jnp.zeros((1, LANES), F32))
        gtok_ref[:, sl] = acc.astype(BF)
        tail_ref[:, sl] = acc[rows - HALO : rows]
        gshort_ref[:, sl] = jnp.concatenate(sums, axis=0)
        return carry

    lax.fori_loop(0, blocks, short_block, 0)


def reduce_kernel(n_dp, n_seq, x_ref, y_ref, got_dp, half, got_seq, full, s1, r1, s2, r2, s3, r3, s4, r4):
    dp = lax.axis_index("dp")
    seq = lax.axis_index("seq")
    mesh_id = pl.DeviceIdType.MESH

    def dp_peer(k):
        return (lax.rem(dp + k, n_dp), seq)

    def seq_peer(k):
        return (dp, lax.rem(seq + k, n_seq))

    barrier = pltpu.get_barrier_semaphore()
    for k in range(1, n_dp):
        pl.semaphore_signal(barrier, inc=1, device_id=dp_peer(k), device_id_type=mesh_id)
    for k in range(1, n_seq):
        pl.semaphore_signal(barrier, inc=1, device_id=seq_peer(k), device_id_type=mesh_id)
    pl.semaphore_wait(barrier, n_dp + n_seq - 2)

    def exchange(count, peer, source, target, send, recv):
        copies = []
        for k in range(1, count):
            copy = pltpu.make_async_remote_copy(
                src_ref=source(k), dst_ref=target(k), send_sem=send.at[k - 1],
                recv_sem=recv.at[k - 1], device_id=peer(k), device_id_type=mesh_id,
            )
            copy.start()
            copies.append(copy)
        for copy in copies:
            copy.wait()

    exchange(n_dp, dp_peer, lambda k: x_ref.at[lax.rem(dp + k, n_dp)],
             lambda k: got_dp.at[k - 1], s1, r1)
    total = x_ref[dp]
    for k in range(1, n_dp):
        total = total + got_dp[k - 1]
    half[...] = total
    exchange(n_seq, seq_peer, lambda k: half.at[lax.rem(seq + k, n_seq)],
             lambda k: got_seq.at[k - 1], s2, r2)
    total = half[seq]
    for k in range(1, n_seq):
        total = total + got_seq[k - 1]
    full[dp, seq] = total
    exchange(n_seq, seq_peer, lambda k: full.at[dp, seq], lambda k: full.at[dp, seq], s3, r3)
    exchange(n_dp, dp_peer, lambda k: full.at[dp], lambda k: full.at[dp], s4, r4)
    y_ref[...] = full[...]


def line_kernel(n_seq, p_ref, g_ref, out_ref, all_ref, own, pair, from_left, from_right,
                load_sem, pair_send, pair_recv, right_send, right_recv, left_send, left_recv,
                self_sem, line_send, line_recv, near_send, near_recv):
    dp = lax.axis_index("dp")
    seq = lax.axis_index("seq")
    chips = n_seq // 2
    chip, core = lax.div(seq, 2), lax.rem(seq, 2)
    pieces = right_send.shape[1]
    rows = own.shape[1] // pieces
    mesh_id = pl.DeviceIdType.MESH
    ahead = 2

    def at(other_chip, other_core):
        return (dp, other_chip * 2 + other_core)

    sibling = at(chip, 1 - core)
    right = at(lax.rem(chip + 1, chips), core)
    left = at(lax.rem(chip + chips - 1, chips), core)
    barrier = pltpu.get_barrier_semaphore()
    for peer in (sibling, right, left):
        pl.semaphore_signal(barrier, inc=1, device_id=peer, device_id_type=mesh_id)
    pl.semaphore_wait(barrier, 3)

    order = []
    for s in range(chips):
        for c in (chips - 1 - s, s):
            if c not in order:
                order.append(c)
    swaps, loads = {}, {}
    for c in order:
        swaps[c] = pltpu.make_async_remote_copy(
            src_ref=p_ref.at[c, 1 - core], dst_ref=pair.at[c], send_sem=pair_send.at[c],
            recv_sem=pair_recv.at[c], device_id=sibling, device_id_type=mesh_id,
        )
        swaps[c].start()
        loads[c] = pltpu.make_async_copy(p_ref.at[c, core], own.at[c], load_sem.at[c])
        loads[c].start()

    def piece(k):
        return pl.ds(k * rows, rows)

    keep = pltpu.make_async_copy(g_ref, all_ref.at[chip, core], self_sem)
    keep.start()

    def source(rightward, s):
        return chip - s if rightward else chip + s

    def holds(rightward, s):
        return source(rightward, s) >= 0 if rightward else source(rightward, s) < chips

    def passes(rightward):
        return chip < chips - 1 if rightward else chip > 0

    def block(rightward, s, k):
        if s == 0:
            return g_ref.at[piece(k)]
        return all_ref.at[source(rightward, s), core, piece(k)]

    def along(rightward, s, k):
        way = 0 if rightward else 1
        return pltpu.make_async_remote_copy(
            src_ref=block(rightward, s, k),
            dst_ref=all_ref.at[source(rightward, s), core, piece(k)],
            send_sem=line_send.at[way, s, k], recv_sem=line_recv.at[way, s, k],
            device_id=right if rightward else left, device_id_type=mesh_id,
        )

    def across(rightward, s, k):
        way = 0 if rightward else 1
        return pltpu.make_async_remote_copy(
            src_ref=block(rightward, s, k),
            dst_ref=all_ref.at[source(rightward, s), core, piece(k)],
            send_sem=near_send.at[way, s, k], recv_sem=near_recv.at[way, s, k],
            device_id=sibling, device_id_type=mesh_id,
        )

    def gather_step(s, k):
        for rightward in (True, False):

            @pl.when(holds(rightward, s))
            def _():
                if s > 0:
                    along(rightward, s - 1, k).wait_recv()
                if s < chips - 1:

                    @pl.when(passes(rightward))
                    def _():
                        along(rightward, s, k).start()

                if s > 0 or rightward:
                    across(rightward, s, k).start()

    def gather_end(s, k):
        for rightward in (True, False):

            @pl.when(holds(rightward, s))
            def _():
                if s < chips - 1:

                    @pl.when(passes(rightward))
                    def _():
                        along(rightward, s, k).wait_send()

                if s > 0 or rightward:
                    across(rightward, s, k).wait()

    def hop(rightward, c, k):
        send, recv, dst, peer = (
            (right_send, right_recv, from_left, right)
            if rightward
            else (left_send, left_recv, from_right, left)
        )
        return pltpu.make_async_remote_copy(
            src_ref=own.at[c, piece(k)], dst_ref=dst.at[c, piece(k)], send_sem=send.at[c, k],
            recv_sem=recv.at[c, k], device_id=peer, device_id_type=mesh_id,
        )

    steps = [(s, k) for s in range(chips - 1) for k in range(pieces)]
    ready = set()

    def target(rightward, s):
        return chips - 1 - s if rightward else s

    def valid(rightward, s):
        return target(rightward, s) > chip if rightward else target(rightward, s) < chip

    for n, (s, k) in enumerate(steps):
        for rightward in (True, False):
            c = target(rightward, s)
            if c not in ready:
                ready.add(c)
                loads[c].wait()
                swaps[c].wait()

            @pl.when(valid(rightward, s))
            def _():
                sl = piece(k)
                inbox = from_left if rightward else from_right
                inner = chip > 0 if rightward else chip < chips - 1
                both = own[c, sl].astype(F32) + pair[c, sl].astype(F32)

                @pl.when(inner)
                def _():
                    hop(rightward, c, k).wait_recv()
                    own[c, sl] = (both + inbox[c, sl].astype(F32)).astype(BF)

                @pl.when(jnp.logical_not(inner))
                def _():
                    own[c, sl] = both.astype(BF)

                if n >= ahead:
                    before, piece_before = steps[n - ahead]
                    hop(rightward, target(rightward, before), piece_before).wait_send()
                hop(rightward, c, k).start()

        gather_step(s, k)

    for k in range(pieces):
        gather_step(chips - 1, k)
    for c in order:
        if c not in ready:
            ready.add(c)
            loads[c].wait()
            swaps[c].wait()
    for c in range(chips):

        @pl.when(chip == c)
        def _():
            for k in range(pieces):
                sl = piece(k)
                out_ref[sl, :] = own[c, sl].astype(F32) + pair[c, sl].astype(F32)
                if c > 0:
                    hop(True, c, k).wait_recv()
                    out_ref[sl, :] += from_left[c, sl].astype(F32)
                if c < chips - 1:
                    hop(False, c, k).wait_recv()
                    out_ref[sl, :] += from_right[c, sl].astype(F32)
            for rightward in (True, False):
                sent = chips - 1 - c if rightward else c
                count = sent * pieces
                for n in range(max(0, count - ahead), count):
                    s, k = steps[n]
                    hop(rightward, target(rightward, s), k).wait_send()

    for s in range(chips):
        for k in range(pieces):
            gather_end(s, k)
    keep.wait()


def sum_and_gather(partial, gated):
    n_seq = lax.axis_size("seq")
    chips = n_seq // 2
    row_count, channels = gated.shape
    pieces = max(1, row_count // 32)
    dma = pltpu.SemaphoreType.DMA
    slots = pltpu.VMEM((chips, row_count, channels), BF)
    return pl.pallas_call(
        functools.partial(line_kernel, n_seq),
        out_shape=[
            jax.ShapeDtypeStruct((row_count, channels), F32),
            jax.ShapeDtypeStruct((chips, 2, row_count, channels), BF),
        ],
        in_specs=[pl.BlockSpec(memory_space=pl.ANY)] * 2,
        out_specs=[pl.BlockSpec(memory_space=pltpu.VMEM), pl.BlockSpec(memory_space=pl.ANY)],
        scratch_shapes=[
            slots, slots, slots, slots,
            dma((chips,)), dma((chips,)), dma((chips,)),
            dma((chips, pieces)), dma((chips, pieces)),
            dma((chips, pieces)), dma((chips, pieces)),
            dma, dma((2, chips, pieces)), dma((2, chips, pieces)),
            dma((2, chips, pieces)), dma((2, chips, pieces)),
        ],
        compiler_params=pltpu.CompilerParams(
            collective_id=1, has_side_effects=True, vmem_limit_bytes=48 << 20
        ),
        cost_estimate=pl.CostEstimate(
            flops=8 * row_count * channels, bytes_accessed=300_000_000, transcendentals=0
        ),
    )(partial.reshape(chips, 2, row_count, channels), gated)


def all_reduce_small(flat):
    n_dp, n_seq = lax.axis_size("dp"), lax.axis_size("seq")
    devices = n_dp * n_seq
    size = flat.shape[0]
    per = -(-size // (devices * 8 * LANES)) * 8
    padded = jnp.pad(flat, (0, devices * per * LANES - size))
    x = padded.reshape(n_dp, n_seq, per, LANES)
    dma = pltpu.SemaphoreType.DMA
    out = pl.pallas_call(
        functools.partial(reduce_kernel, n_dp, n_seq),
        out_shape=jax.ShapeDtypeStruct(x.shape, F32),
        in_specs=[pl.BlockSpec(memory_space=pltpu.VMEM)],
        out_specs=pl.BlockSpec(memory_space=pltpu.VMEM),
        scratch_shapes=[
            pltpu.VMEM((n_dp - 1, n_seq, per, LANES), F32),
            pltpu.VMEM((n_seq, per, LANES), F32),
            pltpu.VMEM((n_seq - 1, per, LANES), F32),
            pltpu.VMEM(x.shape, F32),
            dma((n_dp - 1,)), dma((n_dp - 1,)),
            dma((n_seq - 1,)), dma((n_seq - 1,)),
            dma((n_seq - 1,)), dma((n_seq - 1,)),
            dma((n_dp - 1,)), dma((n_dp - 1,)),
        ],
        compiler_params=pltpu.CompilerParams(
            collective_id=0, has_side_effects=True, vmem_limit_bytes=16 << 20
        ),
        cost_estimate=pl.CostEstimate(flops=size, bytes_accessed=8 * size, transcendentals=0),
    )(x)
    return out.reshape(-1)[:size]


def shards(tokens_in, short_filter, long_filter, out_weight, cotangent):
    tokens = tokens_in[0]
    row_count = tokens.shape[0]
    channels = tokens.shape[1] // 3
    short_taps = short_filter.shape[0]
    group_count, tap_count = long_filter.shape
    per = LANES * group_count // channels
    width = min(1024, channels)
    nb = channels // width
    groups = group_count // nb
    limit = 40 << 20

    weights = lax.all_gather(out_weight, "dp", axis=0, tiled=True)
    upstream = cotangent[0]
    rim = shifted(tokens[row_count - HALO :], "seq", 1).astype(F32)
    filt = long_filter.astype(F32)
    turned = jnp.roll(filt[:, ::-1], 1, axis=1)

    by_part = lambda rows: pl.BlockSpec((rows, width), lambda j, p: (0, p * nb + j))
    features, mixer_in = pl.pallas_call(
        features_kernel,
        grid=(nb, 3),
        in_specs=[by_part(row_count), by_part(HALO), by_part(short_taps)],
        out_specs=[by_part(row_count), pl.BlockSpec((row_count, width), lambda j, p: (0, j))],
        out_shape=[
            jax.ShapeDtypeStruct((row_count, 3 * channels), F32),
            jax.ShapeDtypeStruct((row_count, channels), BF),
        ],
        scratch_shapes=[
            pltpu.VMEM((row_count + HALO, LANES), F32),
            pltpu.VMEM((row_count, width), F32),
        ],
        compiler_params=pltpu.CompilerParams(vmem_limit_bytes=limit),
        cost_estimate=pl.CostEstimate(
            flops=42 * row_count * channels, bytes_accessed=20 * row_count * channels, transcendentals=0
        ),
    )(tokens, rim, short_filter)
    lead = shifted(mixer_in, "seq", 1)

    col = lambda off: pl.BlockSpec((row_count, width), lambda j: (0, off * nb + j))
    mixed, gated = pl.pallas_call(
        functools.partial(mixed_kernel, per),
        grid=(nb,),
        in_specs=[col(0), col(0), col(0), pl.BlockSpec((groups, tap_count), lambda j: (j, 0))],
        out_specs=[col(0), col(0)],
        out_shape=[
            jax.ShapeDtypeStruct((row_count, channels), F32),
            jax.ShapeDtypeStruct((row_count, channels), BF),
        ],
        scratch_shapes=[
            pltpu.VMEM((per * tap_count, 2 * tap_count), BF),
            pltpu.VMEM((2 * tap_count, LANES), BF),
        ],
        compiler_params=pltpu.CompilerParams(vmem_limit_bytes=limit),
        cost_estimate=pl.CostEstimate(
            flops=4 * per * tap_count * row_count * channels,
            bytes_accessed=14 * row_count * channels, transcendentals=0,
        ),
    )(mixer_in, lead, features, turned)

    grad_gated, all_rows = sum_and_gather(
        lax.dot_general(
            upstream, weights, (((1,), (1,)), ((), ())), preferred_element_type=F32
        ).astype(BF),
        gated,
    )
    all_rows = all_rows.reshape(-1, channels)
    weight_grad = lax.dot_general(
        all_rows, upstream, (((0,), (0,)), ((), ())), preferred_element_type=F32
    )
    grad_weight = lax.psum_scatter(
        weight_grad.astype(BF), "dp", scatter_dimension=0, tiled=True
    ).astype(F32)
    output = jnp.dot(all_rows, weights, preferred_element_type=F32).astype(BF)

    grad_mixed_in = (grad_gated * features[:, :channels]).astype(BF)
    grad_next = shifted(grad_mixed_in, "seq", -1)
    at = lambda off: pl.BlockSpec((row_count, width), lambda j, p: (0, off * nb + j))
    group_spec = pl.BlockSpec((groups, tap_count), lambda j, p: (j, 0))
    grad_tokens, tail, head, short_local, long_local = pl.pallas_call(
        functools.partial(backward_kernel, per),
        grid=(nb, 3),
        in_specs=[
            at(0), at(0), at(0), at(1), at(2), at(0), at(0), at(0), group_spec,
            by_part(row_count), by_part(HALO), by_part(short_taps),
        ],
        out_specs=[by_part(row_count), by_part(HALO), by_part(HALO), by_part(HALO), group_spec],
        out_shape=[
            jax.ShapeDtypeStruct((row_count, 3 * channels), BF),
            jax.ShapeDtypeStruct((HALO, 3 * channels), F32),
            jax.ShapeDtypeStruct((HALO, 3 * channels), F32),
            jax.ShapeDtypeStruct((HALO, 3 * channels), F32),
            jax.ShapeDtypeStruct((group_count, tap_count), F32),
        ],
        scratch_shapes=[
            pltpu.VMEM((per * tap_count, 2 * tap_count), BF),
            pltpu.VMEM((2 * tap_count, LANES), BF),
            pltpu.VMEM((per * row_count, LANES), BF),
            pltpu.VMEM((3, row_count + HALO, width), F32),
            pltpu.VMEM((row_count + HALO, LANES), F32),
        ],
        compiler_params=pltpu.CompilerParams(vmem_limit_bytes=limit),
        cost_estimate=pl.CostEstimate(
            flops=8 * per * tap_count * row_count * channels,
            bytes_accessed=40 * row_count * channels, transcendentals=0,
        ),
    )(
        grad_gated, grad_next, features, features, features, mixed, mixer_in, lead, filt,
        tokens, rim, short_filter,
    )

    follow = shifted(head.astype(BF), "seq", -1).astype(F32)
    beyond = jnp.concatenate([jnp.zeros_like(follow), follow], axis=0)
    for j in range(short_taps):
        tail = tail + short_filter[j] * beyond[j : j + HALO]
    grad_tokens = lax.dynamic_update_slice(grad_tokens, tail.astype(BF), (row_count - HALO, 0))

    summed = all_reduce_small(
        jnp.concatenate([short_local.reshape(-1), long_local.reshape(-1)])
    )
    cut = HALO * 3 * channels
    grad_short = summed[:cut].reshape(HALO, 3 * channels)[:short_taps]
    grad_long = summed[cut:].reshape(group_count, tap_count)[:, ::-1]
    return (output[None], grad_tokens[None], grad_short, grad_long, grad_weight)


def solution(mesh):
    return jax.shard_map(
        shards,
        mesh=mesh,
        in_specs=(P("dp", "seq", None), P(), P(), P("dp", "seq"), P("dp", None, "seq")),
        out_specs=(P("dp", None, "seq"), P("dp", "seq", None), P(), P(), P("dp", "seq")),
        check_vma=False,
    )
```
